32 devices in a mesh: lat: 8 (over z, y), lon: 4 (over x, core).
Axes of the slice: x: 2, y: 2, z: 4, core: 2. Of those that a mesh axis runs over, the one named last changes fastest.
Arguments:
- spec: float32 [4, 2, 640, 1344], P(None, None, 'lat', 'lon'), may hold values from -6 to 6
- legendre: bfloat16 [640, 1344, 1280], P('lat', 'lon'), may hold values from -0.25 to 0.25
- wave_pairs: int32 [640], replicated, may hold values from 0 to 639, each once
- row_waves: int32 [2560], P('lat'), may hold values from 16 to 1280, as said below
- forcing: float32 [4, 2560, 5120], P(None, 'lat', 'lon'), may hold values from -6 to 6
- helm_coef: float32 [4], replicated, may hold values from 6.1035155e-07 to 4.8828124e-06
Outputs:
- grid_field: float32 [4, 2560, 5120], P(None, 'lat', 'lon')
- spec_new: float32 [4, 2, 640, 1344], P(None, None, 'lat', 'lon')
The draws below stay inside these ranges and needn't reach their ends.
Inputs may be any that keep to these rules, and one draw needn't show every extreme that they name: Each value appears once; row s holds the wavenumbers wave_pairs[s] and 1279 - wave_pairs[s]. `row_waves`: rows near the equator resolve all 1280 wavenumbers.
All inputs are finite; a program needn't handle non-finite values.
Results may differ from the reference program's by a relative error of at most 0.028.
Values may be sent and summed in bfloat16 or wider, within the bound.
No kernel may reach another device: no remote copies, remote signals or barrier semaphores. Data moves between devices by JAX's collectives and lax.ppermute only.
A program may use at most 192 MiB of HBM per device.

```python
import math
import jax
import jax.numpy as jnp
from jax import lax

M = 1280
NLAT = 2560
NLON = 5120
F = 4
PAIRS = 640
NPAD = 1344
N_LON = 4


def draw_row_waves(key, part):
    row_index = jnp.arange(NLAT, dtype=jnp.int32)
    pole_gap = jnp.minimum(row_index, NLAT - 1 - row_index)
    jitter = jax.random.randint(key, (NLAT,), 0, M // 4, dtype=jnp.int32)
    jitter = jnp.where(pole_gap == 0, 0, jitter)
    return jnp.minimum(M, 16 + 2 * pole_gap * M // NLAT + jitter).astype(jnp.int32)


def levels(own_key, extent, split, smallest, high):
    level, own = 1.0, jax.random.fold_in(own_key, 6)
    for dim, parts in split:
        draws = jnp.exp(jax.random.uniform(jax.random.fold_in(own, dim), (parts,), jnp.float32, smallest / len(split), high / len(split)))
        level = level * jnp.repeat(draws, extent[dim] // parts).reshape([-1 if axis == dim else 1 for axis in range(len(extent))])
    return level


def centred(key, extent, deviation, most, shards=(), held_as=jnp.bfloat16):
    drawn = deviation * jax.random.normal(key, extent, jnp.float32)
    if shards:
        drawn = drawn * levels(key, extent, shards, -0.22, 0.18)
    return jnp.clip(drawn, -most, most).astype(held_as)


def setup_inputs(seed: int = 0) -> dict:
    keys = jax.random.split(jax.random.key(seed), 7)
    return {
        "spec": centred(keys[0], (F, 2, PAIRS, NPAD), 1.0, 6.0, ((2, 8), (3, 4)), jnp.float32),
        "legendre": centred(keys[1], (PAIRS, NPAD, NLAT // 2), (M // 2) ** -0.5, 0.25, ((0, 8), (1, 4))),
        "wave_pairs": jax.random.permutation(keys[2], PAIRS).astype(jnp.int32),
        "row_waves": draw_row_waves(jax.random.fold_in(keys[6], 71), 0),
        "forcing": centred(keys[4], (F, NLAT, NLON), 1.0, 6.0, ((1, 8), (2, 4)), jnp.float32),
        "helm_coef": jnp.clip(jnp.exp(jax.random.uniform(keys[5], (F,), jnp.float32, math.log(6.103515488575795e-07), math.log(4.882812390860636e-06))), 6.103515488575795e-07, 4.882812390860636e-06),
    }


def column_info(pair_values, columns):
    boundary = M - pair_values[:, None]
    first_part = columns[None, :] < boundary
    valid_cols = columns[None, :] < M + 1
    second_part = jnp.logical_and(valid_cols, jnp.logical_not(first_part))
    offset = jnp.where(first_part, columns[None, :], columns[None, :] - boundary)
    parity = (1 - 2 * (offset % 2)).astype(jnp.float32)
    degree = jnp.where(first_part, pair_values[:, None] + columns[None, :], columns[None, :] - 1)
    return (first_part.astype(jnp.float32), second_part.astype(jnp.float32), parity, degree.astype(jnp.float32))

def wave_numbers(pair_values):
    return jnp.stack([pair_values, M - 1 - pair_values], axis=-1)

def angles(wave_table, positions, length):
    winding = wave_table[..., None] * positions % length
    return winding.astype(jnp.float32) * (2.0 * math.pi / length)

def reference(spec, legendre, wave_pairs, row_waves, forcing, helm_coef):
    columns = jnp.arange(NPAD, dtype=jnp.int32)
    first_part, second_part, parity, degree = column_info(wave_pairs, columns)
    up_scale = 0.5 / math.sqrt(M)
    half_lats = NLAT // 2
    col_width = NPAD // N_LON
    coefficients = jnp.transpose(spec.astype(jnp.bfloat16), (2, 0, 1, 3))

    def inverse_slot(inputs):
        basis, values, part_one, part_two, signs = inputs
        selector = jnp.stack([part_one, part_two])
        flip_signs = jnp.stack([jnp.ones_like(signs), signs])
        factor = selector[:, None, :] * flip_signs[None, :, :]
        mixed_terms = factor[:, :, None, None, :] * values.astype(jnp.float32)[None, None]
        mixed_terms = mixed_terms.reshape(2, 2, F, 2, N_LON, col_width)
        blocks = basis.astype(jnp.float32).reshape(N_LON, col_width, half_lats)
        term_sums = jnp.einsum('qhfrgc,gck->gqhfrk', mixed_terms, blocks) * up_scale
        term_sums = lax.optimization_barrier(term_sums.astype(jnp.bfloat16)).astype(jnp.float32)
        return lax.optimization_barrier(jnp.sum(term_sums, axis=0))
    slot_sums = lax.map(inverse_slot, (legendre, coefficients, first_part, second_part, parity))
    north_half = slot_sums[:, :, 0]
    south_half = jnp.flip(slot_sums[:, :, 1], axis=-1)
    fourier = jnp.concatenate([north_half, south_half], axis=-1)
    wave_table = wave_numbers(wave_pairs)
    kept_mask = (wave_table[:, :, None] < row_waves[None, None, :]).astype(jnp.float32)
    fourier = (fourier * kept_mask[:, :, None, None, :]).astype(jnp.bfloat16)
    positions = jnp.arange(NLON, dtype=jnp.int32)
    phases = angles(wave_table, positions, NLON)
    weight = jnp.where(wave_table == 0, 1.0, 2.0).astype(jnp.float32)[..., None]
    forward_table = jnp.stack([weight * jnp.cos(phases), -weight * jnp.sin(phases)]).astype(jnp.bfloat16)
    grid_field = jnp.einsum('pqfrl,rpqx->flx', fourier.astype(jnp.float32), forward_table.astype(jnp.float32))
    tendency = (forcing - 0.5 * grid_field * grid_field).astype(jnp.bfloat16)
    back_table = (jnp.stack([jnp.cos(phases), -jnp.sin(phases)]) / NLON).astype(jnp.bfloat16)
    seg_width = NLON // N_LON
    tend_blocks = jnp.transpose(tendency.reshape(F, NLAT, N_LON, seg_width), (2, 0, 1, 3))
    back_blocks = jnp.transpose(back_table.reshape(2, PAIRS, 2, N_LON, seg_width), (3, 0, 1, 2, 4))

    def add_segment(running, inputs):
        tend_piece, back_piece = inputs
        segment = jnp.einsum('flx,rpqx->pqfrl', tend_piece.astype(jnp.float32), back_piece.astype(jnp.float32))
        segment = lax.optimization_barrier(segment.astype(jnp.bfloat16)).astype(jnp.float32)
        return (running + segment, None)
    analysis, _ = lax.scan(add_segment, jnp.zeros((PAIRS, 2, F, 2, NLAT), jnp.float32), (tend_blocks, back_blocks))
    fan = (analysis * kept_mask[:, :, None, None, :]).astype(jnp.bfloat16)
    down_scale = math.sqrt(M)

    def direct_slot(inputs):
        basis, values, part_one, part_two, signs = inputs
        north_half = values[..., :half_lats]
        south_half = jnp.flip(values[..., half_lats:], axis=-1)
        mixed_terms = jnp.stack([north_half, south_half], axis=1).astype(jnp.float32)
        products = jnp.einsum('qhfrk,ck->qhfrc', mixed_terms, basis.astype(jnp.float32))
        result_cols = part_one * (products[0, 0] + signs * products[0, 1]) + part_two * (products[1, 0] + signs * products[1, 1])
        return result_cols * down_scale
    spectral_tendency = lax.map(direct_slot, (legendre, fan, first_part, second_part, parity))
    spectral_tendency = jnp.transpose(spectral_tendency, (1, 2, 0, 3))
    valid_cols = first_part + second_part
    divisor = 1.0 + helm_coef[:, None, None, None] * (degree * (degree + 1.0))[None, None]
    spec_new = valid_cols[None, None] * (spec + spectral_tendency) / divisor
    return (grid_field, spec_new)
```

```python
import math

import jax
import jax.numpy as jnp
from jax import lax
from jax.experimental import pallas as pl
from jax.experimental.pallas import tpu as pltpu
from jax.sharding import PartitionSpec as P

M = 1280
LANES = 128
HALF = LANES // 2
STEP = 16
VMEM_BYTES = 50 * 1024 * 1024
F32 = jnp.float32
BF16 = jnp.bfloat16


def column_info(pair_values, columns):
    boundary = M - pair_values[:, None]
    first_part = columns[None, :] < boundary
    valid_cols = columns[None, :] < M + 1
    second_part = jnp.logical_and(valid_cols, jnp.logical_not(first_part))
    offset = jnp.where(first_part, columns[None, :], columns[None, :] - boundary)
    parity = (1 - 2 * (offset % 2)).astype(jnp.float32)
    degree = jnp.where(first_part, pair_values[:, None] + columns[None, :], columns[None, :] - 1)
    return (
        first_part.astype(jnp.float32),
        second_part.astype(jnp.float32),
        parity,
        degree.astype(jnp.float32),
    )


def wave_numbers(pair_values):
    return jnp.stack([pair_values, M - 1 - pair_values], axis=-1)


def angles(wave_table, positions, length):
    winding = wave_table[..., None] * positions % length
    return winding.astype(jnp.float32) * (2.0 * math.pi / length)


def plain_body(spec, legendre, wave_pairs, row_waves, forcing, helm_coef):
    groups = lax.axis_size("lat")
    lat_id = lax.axis_index("lat")
    lon_id = lax.axis_index("lon")
    fields, _, slot_count, col_width = spec.shape
    half_lats = legendre.shape[2]
    lats_total = 2 * half_lats
    band_rows = row_waves.shape[0]
    seg_width = forcing.shape[2]
    lons_total = seg_width * lax.axis_size("lon")
    my_pairs = lax.dynamic_slice_in_dim(wave_pairs, lat_id * slot_count, slot_count)
    columns = lon_id * col_width + jnp.arange(col_width, dtype=jnp.int32)
    first_part, second_part, parity, degree = column_info(my_pairs, columns)
    selector = jnp.stack([first_part, second_part])
    flip_signs = jnp.stack([jnp.ones_like(parity), parity])
    factor = (selector[:, None] * flip_signs[None]).astype(jnp.bfloat16)
    mixed_terms = factor[:, :, None, None] * spec.astype(jnp.bfloat16)[None, None]
    upward = jnp.einsum(
        "qhfrsc,sck->hkfrsq", mixed_terms, legendre, preferred_element_type=jnp.float32
    ) * (0.5 / math.sqrt(M))
    lat_rows = jnp.concatenate([upward[0], jnp.flip(upward[1], axis=0)], axis=0)
    partial_value = lat_rows.reshape(lats_total, -1).astype(jnp.bfloat16)
    wave_table = wave_numbers(wave_pairs).reshape(groups, slot_count * 2)
    kept_mask = (wave_table[None, :, None, None, :] < row_waves[:, None, None, None, None]).astype(
        jnp.float32
    )
    shares = lax.psum_scatter(
        partial_value.astype(jnp.float32).astype(jnp.bfloat16),
        "lon",
        scatter_dimension=1,
        tiled=True,
    )
    banded = lax.all_to_all(shares, "lat", split_axis=0, concat_axis=1, tiled=True)
    whole = lax.all_gather(banded.reshape(band_rows, groups, -1), "lon", axis=2, tiled=True)
    fourier = whole.reshape(band_rows, groups, fields, 2, slot_count * 2) * kept_mask.astype(
        jnp.bfloat16
    )
    places = lon_id * seg_width + jnp.arange(seg_width, dtype=jnp.int32)
    phases = angles(wave_table, places, lons_total)
    weight = jnp.where(wave_table == 0, 1.0, 2.0).astype(jnp.float32)[..., None]
    forward_table = jnp.stack([weight * jnp.cos(phases), -weight * jnp.sin(phases)]).astype(
        jnp.bfloat16
    )
    grid_field = jnp.einsum(
        "lgfrn,rgnx->flx", fourier, forward_table, preferred_element_type=jnp.float32
    )
    tendency = (forcing - 0.5 * grid_field * grid_field).astype(jnp.bfloat16)
    back_table = (jnp.stack([jnp.cos(phases), -jnp.sin(phases)]) / lons_total).astype(jnp.bfloat16)
    pieces = jnp.einsum("flx,rgnx->lgfrn", tendency, back_table, preferred_element_type=jnp.float32)
    pieces = (pieces * kept_mask).astype(jnp.bfloat16)
    shares_back = lax.psum_scatter(
        pieces.reshape(band_rows, groups, -1).astype(jnp.float32).astype(jnp.bfloat16),
        "lon",
        scatter_dimension=2,
        tiled=True,
    )
    swapped = lax.all_to_all(shares_back, "lat", split_axis=1, concat_axis=0, tiled=True)
    fan_flat = lax.all_gather(swapped, "lon", axis=2, tiled=True).reshape(lats_total, -1)
    fan_rows = fan_flat.reshape(lats_total, fields, 2, slot_count, 2)
    mixed_back = jnp.stack([fan_rows[:half_lats], jnp.flip(fan_rows[half_lats:], axis=0)])
    downward = jnp.einsum(
        "hkfrsq,sck->frsqhc", mixed_back, legendre, preferred_element_type=jnp.float32
    )
    spectral_tendency = (
        first_part * (downward[:, :, :, 0, 0] + parity * downward[:, :, :, 0, 1])
        + second_part * (downward[:, :, :, 1, 0] + parity * downward[:, :, :, 1, 1])
    ) * math.sqrt(M)
    valid_cols = first_part + second_part
    divisor = 1.0 + helm_coef[:, None, None, None] * (degree * (degree + 1.0))[None, None]
    spec_new = valid_cols[None, None] * (spec + spectral_tendency) / divisor
    return (grid_field, spec_new)


def row_of(h, q, d, r):
    return ((h * 2 + q) * 4 + d) * 2 + r


def dot(a, b):
    return jnp.dot(a, b, preferred_element_type=F32)


def dot_nt(a, b):
    return lax.dot_general(a, b, (((1,), (1,)), ((), ())), preferred_element_type=F32)


def low_half():
    return lax.broadcasted_iota(jnp.int32, (STEP, LANES), 1) < HALF


def tile_groups(tiles, packed, groups):
    if packed:
        return [(n, 2 * n) for n in range(len(tiles))]
    return [(n, n) for n in range(len(tiles))]


def up_kernel(place, mix, *refs, tiles, packed, groups, scale):
    legs, (keep, send, scratch) = refs[: len(tiles)], refs[len(tiles) :]
    me = place[0]
    rows = mix.shape[1]
    for s in range(STEP):
        basis = jnp.concatenate([leg[s] for leg in legs], axis=1)
        found = dot(mix[s], basis) * scale
        for n in range(len(tiles)):
            scratch[n, s * rows : (s + 1) * rows, :] = found[:, n * LANES : (n + 1) * LANES]

    def fetch(h, q, d, r, n):
        return scratch[n, pl.ds(row_of(h, q, d, r), STEP, stride=rows), :]

    for h in range(2):
        for q in range(2):
            for d in range(4):
                target = (keep, send)[d % 2]
                for n, group in tile_groups(tiles, packed, groups):
                    slot = me ^ (groups - 1 - group if h else group)
                    if packed:
                        real, imag = fetch(h, q, d, 0, n), fetch(h, q, d, 1, n)
                        even = jnp.where(low_half(), real, pltpu.roll(imag, HALF, 1))
                        odd = jnp.where(low_half(), pltpu.roll(real, HALF, 1), imag)
                        target[d // 2, slot, q] = even.astype(BF16)
                        target[d // 2, slot ^ 1, q] = odd.astype(BF16)
                    else:
                        for r in range(2):
                            target[d // 2, slot, r, q] = fetch(h, q, d, r, n).astype(BF16)


def up_chunk(place, mix, legendre, tiles, packed, groups, scale):
    slots, rows, width = mix.shape
    lead = (2, groups, 2) if packed else (2, groups, 2, 2)
    out = jax.ShapeDtypeStruct(lead + (slots, LANES), BF16)
    out_spec = pl.BlockSpec(lead + (STEP, LANES), lambda i, p: (0,) * len(lead) + (i, 0))

    def leg_spec(tile):
        return pl.BlockSpec((STEP, width, LANES), lambda i, p: (i, 0, tile))

    return pl.pallas_call(
        lambda *refs: up_kernel(*refs, tiles=tiles, packed=packed, groups=groups, scale=scale),
        out_shape=(out, out),
        grid_spec=pltpu.PrefetchScalarGridSpec(
            num_scalar_prefetch=1,
            grid=(slots // STEP,),
            in_specs=[pl.BlockSpec((STEP, rows, width), lambda i, p: (i, 0, 0))]
            + [leg_spec(t) for t in tiles],
            out_specs=(out_spec, out_spec),
            scratch_shapes=[pltpu.VMEM((len(tiles), STEP * rows, LANES), F32)],
        ),
        compiler_params=pltpu.CompilerParams(vmem_limit_bytes=VMEM_BYTES),
        cost_estimate=pl.CostEstimate(
            flops=2 * slots * 256 * 2 * width * len(tiles) * LANES // 2,
            bytes_accessed=slots * width * len(tiles) * LANES * 2,
            transcendentals=0,
        ),
        name="legendre_up",
    )(place, mix, *[legendre] * len(tiles))


def down_kernel(place, *refs, tiles, packed, groups, first, last):
    fans, legs = refs[:4], refs[4 : 4 + len(tiles)]
    rest = list(refs[4 + len(tiles) :])
    factors = rest.pop(0)
    previous = None if first else rest.pop(0)
    spec, inverse = (rest.pop(0), rest.pop(0)) if last else (None, None)
    out, scratch, sums = rest
    me, mine = place[0], place[1]
    rows = 32

    def put(h, q, d, r, n, value):
        scratch[n, pl.ds(row_of(h, q, d, r), STEP, stride=rows), :] = value

    for h in range(2):
        for q in range(2):
            for d in range(4):
                for n, group in tile_groups(tiles, packed, groups):
                    slot = me ^ (groups - 1 - group if h else group)
                    if packed:
                        even = fans[d][slot, q].astype(F32)
                        odd = fans[d][slot ^ 1, q].astype(F32)
                        put(h, q, d, 0, n, jnp.where(low_half(), even, pltpu.roll(odd, HALF, 1)))
                        put(h, q, d, 1, n, jnp.where(low_half(), pltpu.roll(even, HALF, 1), odd))
                    else:
                        for r in range(2):
                            put(h, q, d, r, n, fans[d][slot, r, q].astype(F32))
    for s in range(STEP):
        basis = jnp.concatenate([leg[s] for leg in legs], axis=1)
        values = [scratch[n, s * rows : (s + 1) * rows, :] for n in range(len(tiles))]
        values = jnp.concatenate(values, axis=1).astype(BF16)
        found = dot_nt(values, basis)
        total = sum(found[8 * n : 8 * n + 8] * factors[s, n : n + 1, :] for n in range(4))
        for n in range(8):
            sums[n, s : s + 1, :] = total[n : n + 1]
    for d in range(4):
        field = mine ^ d
        for r in range(2):
            n = 2 * d + r
            total = sums[n]
            if not first:
                total = total + previous[field, r]
            if last:
                total = (spec[field, r] + total * math.sqrt(M)) * inverse[field]
            out[field, r] = total


def down_chunk(place, fans, legendre, factors, previous, spec, inverse, tiles, packed, groups):
    slots, _, width = factors.shape
    first, last = previous is None, spec is not None
    lead = (groups, 2) if packed else (groups, 2, 2)
    fan_spec = pl.BlockSpec(lead + (STEP, LANES), lambda i, p: (0,) * len(lead) + (i, 0))
    field_spec = pl.BlockSpec((4, 2, STEP, width), lambda i, p: (0, 0, i, 0))

    def leg_spec(tile):
        return pl.BlockSpec((STEP, width, LANES), lambda i, p: (i, 0, tile))

    operands = [*fans, *[legendre] * len(tiles), factors]
    specs = [fan_spec] * 4 + [leg_spec(t) for t in tiles]
    specs.append(pl.BlockSpec((STEP, 4, width), lambda i, p: (i, 0, 0)))
    if not first:
        operands.append(previous)
        specs.append(field_spec)
    if last:
        operands += [spec, inverse]
        specs += [field_spec, pl.BlockSpec((4, STEP, width), lambda i, p: (0, i, 0))]
    return pl.pallas_call(
        lambda *refs: down_kernel(
            *refs, tiles=tiles, packed=packed, groups=groups, first=first, last=last
        ),
        out_shape=jax.ShapeDtypeStruct((4, 2, slots, width), F32),
        grid_spec=pltpu.PrefetchScalarGridSpec(
            num_scalar_prefetch=1,
            grid=(slots // STEP,),
            in_specs=specs,
            out_specs=field_spec,
            scratch_shapes=[
                pltpu.VMEM((len(tiles), STEP * 32, LANES), F32),
                pltpu.VMEM((8, STEP, width), F32),
            ],
        ),
        compiler_params=pltpu.CompilerParams(vmem_limit_bytes=VMEM_BYTES),
        cost_estimate=pl.CostEstimate(
            flops=2 * slots * 256 * width * len(tiles) * LANES,
            bytes_accessed=slots * width * len(tiles) * LANES * 2,
            transcendentals=0,
        ),
        name="legendre_down",
    )(place, *operands)


def table_kernel(cos_far, sin_far, cos_near, sin_near, out):
    for n in range(cos_far.shape[1]):
        lanes = slice(n * LANES, (n + 1) * LANES)
        cos_a, sin_a = cos_far[:, n : n + 1], sin_far[:, n : n + 1]
        cos_b, sin_b = cos_near[...], sin_near[...]
        out[0, 0, :, lanes] = (cos_a * cos_b - sin_a * sin_b).astype(BF16)
        out[1, 0, :, lanes] = (-sin_a * cos_b - cos_a * sin_b).astype(BF16)


def make_table(waves, first_place, width, length, groups):
    far = angles(waves, first_place + LANES * jnp.arange(width // LANES, dtype=jnp.int32), length)
    near = angles(waves, jnp.arange(LANES, dtype=jnp.int32), length)
    count = waves.shape[0] // groups
    far_spec = pl.BlockSpec((count, width // LANES), lambda i: (i, 0))
    near_spec = pl.BlockSpec((count, LANES), lambda i: (i, 0))
    return pl.pallas_call(
        table_kernel,
        out_shape=jax.ShapeDtypeStruct((2, groups, count, width), BF16),
        grid=(groups,),
        in_specs=[far_spec, far_spec, near_spec, near_spec],
        out_specs=pl.BlockSpec((2, 1, count, width), lambda i: (0, i, 0, 0)),
        compiler_params=pltpu.CompilerParams(vmem_limit_bytes=VMEM_BYTES),
        name="zonal_table",
    )(jnp.cos(far), jnp.sin(far), jnp.cos(near), jnp.sin(near))


def zonal_kernel(place, *refs, packed, first, scale):
    coefs, rest = refs[:4], list(refs[4:])
    table, flip, spread, waves, row_waves, forcing = rest[:6]
    rest = rest[6:] if first else rest[7:]
    grid, keep, send, weight, lines, force, field, tend, read_sem, write_sem = rest
    mine, offset = place[1], pl.multiple_of(place[2], 8)
    parts, groups, per_group, width = table.shape
    count = groups * per_group
    rows = HALF if packed else LANES
    passes = ((1, 3, 0, 2),) if packed else ((1, 3), (0, 2))
    block = 256
    wave_block = groups // 2

    def force_copy(d):
        source = forcing.at[mine ^ d, pl.ds(offset, rows), :]
        return pltpu.make_async_copy(source, force.at[d], read_sem.at[d])

    def grid_copy(d):
        target = grid.at[mine ^ d, pl.ds(offset, rows), :]
        return pltpu.make_async_copy(field.at[d], target, write_sem.at[d])

    for d in range(4):
        force_copy(d).start()
    kept = waves[...] < row_waves[...]
    weight[...] = jnp.where(kept, jnp.where(waves[...] == 0, 1.0, 2.0), 0.0).astype(BF16)
    for fields in passes:
        for n, d in enumerate(fields):
            for r in range(2):
                if packed:
                    values = coefs[d][...].reshape(count, LANES) * weight[...]
                    turn = flip[r]
                else:
                    values = coefs[d][:, r].reshape(count, LANES) * weight[...]
                    turn = flip[...]
                lines[r, n * rows : (n + 1) * rows, :] = dot_nt(turn, values).astype(BF16)
        for d in fields:
            force_copy(d).wait()

        @pl.loop(0, width // block)
        def _(step):
            lanes = pl.ds(pl.multiple_of(step * block, block), block)
            total = dot(lines[0], table[0, :, :, lanes].reshape(count, block))
            total += dot(lines[1], table[1, :, :, lanes].reshape(count, block))
            for n, d in enumerate(fields):
                here = slice(n * rows, (n + 1) * rows)
                part = total[here]
                field[d, :, lanes] = part
                tend[here, lanes] = (force[d, :, lanes] - 0.5 * part * part).astype(BF16)

        for d in fields:
            grid_copy(d).start()

        @pl.loop(0, groups // wave_block)
        def _(step):
            several = pl.ds(step * wave_block, wave_block)
            some = wave_block * per_group
            mask = weight[pl.ds(pl.multiple_of(step * some, some), some), :].astype(F32) > 0
            found = []
            for r in range(2):
                sums = dot_nt(table[r, several].reshape(some, width), tend[...])
                found.append((sums * scale).astype(BF16))
            for n, d in enumerate(fields):
                target = (keep, send)[d % 2]
                if packed:
                    turned = dot(found[0], spread[n, 0]) + dot(found[1], spread[n, 1])
                    turned = jnp.where(mask, turned, 0.0).astype(BF16)
                    target[d // 2, several] = turned.reshape((wave_block,) + target.shape[2:])
                else:
                    for r in range(2):
                        turned = dot(found[r][:, n * rows : (n + 1) * rows], flip[...])
                        turned = jnp.where(mask, turned, 0.0).astype(BF16)
                        target[d // 2, several, r] = turned.reshape(
                            (wave_block,) + target.shape[3:]
                        )

    for d in range(4):
        grid_copy(d).wait()


def zonal_chunk(place, coefs, table, flip, spread, waves, row_waves, forcing, grid, packed, scale):
    parts, groups, per_group, width = table.shape
    count = groups * per_group
    rows = HALF if packed else LANES
    batch = 4 * rows if packed else 2 * rows
    first = grid is None
    sent = jax.ShapeDtypeStruct((2,) + coefs[0].shape, BF16)
    vmem, anywhere = pl.BlockSpec(memory_space=pltpu.VMEM), pl.BlockSpec(memory_space=pl.ANY)
    operands = [place, *coefs, table, flip, spread, waves, row_waves, forcing]
    specs = [pl.BlockSpec(memory_space=pltpu.SMEM)] + [vmem] * 9 + [anywhere]
    aliases = {}
    if not first:
        aliases = {len(operands): 0}
        operands.append(grid)
        specs.append(anywhere)
    return pl.pallas_call(
        lambda *refs: zonal_kernel(*refs, packed=packed, first=first, scale=scale),
        out_shape=(jax.ShapeDtypeStruct(forcing.shape, F32), sent, sent),
        in_specs=specs,
        out_specs=(anywhere, vmem, vmem),
        scratch_shapes=[
            pltpu.VMEM((count, LANES), BF16),
            pltpu.VMEM((2, batch, count), BF16),
            pltpu.VMEM((4, rows, width), F32),
            pltpu.VMEM((4, rows, width), F32),
            pltpu.VMEM((batch, width), BF16),
            pltpu.SemaphoreType.DMA((4,)),
            pltpu.SemaphoreType.DMA((4,)),
        ],
        input_output_aliases=aliases,
        compiler_params=pltpu.CompilerParams(vmem_limit_bytes=VMEM_BYTES),
        cost_estimate=pl.CostEstimate(
            flops=2 * 2 * 2 * 4 * rows * count * width,
            bytes_accessed=2 * 2 * count * width + 2 * 4 * 4 * rows * width,
            transcendentals=0,
        ),
        name="zonal",
    )(*operands)


def swap(value, axis, bit):
    pairs = [(n, n ^ bit) for n in range(lax.axis_size(axis))]
    return lax.ppermute(value, axis, pairs)


def add(*values):
    return sum(v.astype(F32) for v in values).astype(BF16)


def reduce_lon(keep, send):
    other = swap(send, "lon", 1)
    away = swap(add(keep[1], other[1]), "lon", 2)
    return add(keep[0], other[0], away)


def gather_lon(own):
    across = swap(own, "lon", 2)
    return own, swap(own, "lon", 1), across, swap(across, "lon", 1)


def exchange_lat(value, bits):
    value = value[:, None]
    for bit in bits:
        size = value.shape[0] // 2
        arrived = swap(value[size:], "lat", bit)
        value = jnp.stack([value[:size], arrived], axis=1)
        value = value.reshape((size, 2 * value.shape[2]) + value.shape[3:])
    return value[0]


def fast_plan(spec, legendre, row_waves, forcing):
    groups, lon_size = lax.axis_size("lat"), lax.axis_size("lon")
    fields, _, slots, _ = spec.shape
    half_lats, band, width = legendre.shape[2], row_waves.shape[0], forcing.shape[2]
    per_pair, odd = divmod(2 * band, LANES)
    if (groups, lon_size, fields) != (8, 4, 4) or odd or per_pair % 2 == 0:
        return None
    if slots % STEP or half_lats != 4 * band or width % 256 or 2 * slots % STEP:
        return None
    pairs = range(half_lats // (2 * band))
    full = [
        [t for p in pairs for t in (per_pair * p + n, per_pair * (p + 1) - 1 - n)]
        for n in range(per_pair // 2)
    ]
    return [per_pair * p + per_pair // 2 for p in pairs], full


def body(spec, legendre, wave_pairs, row_waves, forcing, helm_coef):
    plan = fast_plan(spec, legendre, row_waves, forcing)
    if plan is None:
        return plain_body(spec, legendre, wave_pairs, row_waves, forcing, helm_coef)
    shared_tiles, full_tiles = plan
    groups = lax.axis_size("lat")
    lat_id, lon_id = lax.axis_index("lat"), lax.axis_index("lon")
    fields, _, slots, col_width = spec.shape
    band, seg_width = row_waves.shape[0], forcing.shape[2]
    length = seg_width * lax.axis_size("lon")
    top = groups // 2
    bits = [1 << n for n in range(groups.bit_length() - 1)]

    my_pairs = lax.dynamic_slice_in_dim(wave_pairs, lat_id * slots, slots)
    columns = lon_id * col_width + jnp.arange(col_width, dtype=jnp.int32)
    first_part, second_part, parity, degree = column_info(my_pairs, columns)
    factors = jnp.stack(
        [first_part, second_part, parity * first_part, parity * second_part], axis=1
    )
    near = jnp.stack([lax.dynamic_index_in_dim(spec, lon_id ^ d, 0, False) for d in range(4)])
    near = jnp.transpose(near.astype(BF16), (2, 0, 1, 3)).reshape(slots, 1, 2 * fields, col_width)
    mix = (factors[:, :, None].astype(BF16) * near).reshape(slots, 8 * fields, col_width)
    divisor = 1.0 + helm_coef[:, None, None] * (degree * (degree + 1.0))[None]
    inverse = (first_part + second_part)[None] / divisor

    positions = [sum(((p >> n) & 1) << (len(bits) - 1 - n) for n in range(len(bits))) for p in range(groups)]
    grouped = wave_pairs.reshape(groups, slots)
    near_pairs = jnp.stack(
        [lax.dynamic_index_in_dim(grouped, lat_id ^ e, 0, False) for e in positions]
    )
    waves = jnp.stack([near_pairs, M - 1 - near_pairs], axis=1).reshape(-1)
    table = make_table(waves, lon_id * seg_width, seg_width, length, groups)

    south = lat_id >= top
    north = jnp.where(south, groups - 1 - lat_id, lat_id)
    row = jnp.arange(LANES, dtype=jnp.int32)
    place = jnp.stack([lat_id, lon_id])
    chunks = [(shared_tiles, True, 0)] + [(t, False, n) for n, t in enumerate(full_tiles)]
    setups = []
    for tiles, packed, n in chunks:
        rows = HALF if packed else LANES
        start = band - rows if packed else n * LANES
        start = jnp.where(north % 2 == 0, start, band - rows - start)
        start = jnp.where(south, band - rows - start, start)
        mirrored = jnp.where(south, rows - 1 - row[:rows], row[:rows])
        if packed:
            target = HALF * jnp.arange(2)[:, None] + mirrored[None]
            flip = target[..., None] == row
            spread = [
                jnp.concatenate([flip[r] if m == k else jnp.zeros_like(flip[r]) for m in range(4)])
                for k in range(4)
                for r in range(2)
            ]
            spread = jnp.stack(spread).reshape(4, 2, 4 * rows, LANES).astype(BF16)
        else:
            flip = mirrored[:, None] == row
            spread = jnp.zeros((8, LANES), BF16)
        kept = lax.dynamic_slice_in_dim(row_waves, start, rows)
        kept = jnp.sum(jnp.where(flip, kept[:, None], 0), axis=tuple(range(flip.ndim - 1)))
        spot = jnp.stack([lat_id, lon_id, start]).astype(jnp.int32)
        setups.append((spot, flip.astype(BF16), spread, kept[None].astype(jnp.int32)))

    scale = 0.5 / math.sqrt(M)
    grid_field, total = None, None
    sums = [up_chunk(place, mix, legendre, t, packed, groups, scale) for t, packed, _ in chunks]
    owns = [exchange_lat(reduce_lon(*s), bits[::-1]) for s in sums]
    fans = []
    for (tiles, packed, _), own, (spot, flip, spread, kept) in zip(chunks, owns, setups):
        coefs = gather_lon(own)
        grid_field, keep, send = zonal_chunk(
            spot, coefs, table, flip, spread, waves[:, None], kept, forcing, grid_field, packed, 1.0 / length
        )
        fans.append(gather_lon(exchange_lat(reduce_lon(keep, send), bits)))
    for n, (tiles, packed, _) in enumerate(chunks):
        last = n == len(chunks) - 1
        total = down_chunk(
            place, fans[n], legendre, factors, total, spec if last else None,
            inverse if last else None, tiles, packed, groups,
        )
    return grid_field, total


def solution(mesh):
    return jax.shard_map(
        body,
        mesh=mesh,
        in_specs=(
            P(None, None, "lat", "lon"),
            P("lat", "lon", None),
            P(),
            P("lat"),
            P(None, "lat", "lon"),
            P(),
        ),
        out_specs=(P(None, "lat", "lon"), P(None, None, "lat", "lon")),
        check_vma=False,
    )
```

```python
import math

import jax
import jax.numpy as jnp
from jax import lax
from jax.experimental import pallas as pl
from jax.experimental.pallas import tpu as pltpu
from jax.sharding import PartitionSpec as P

M = 1280
LANES = 128
HALF = LANES // 2
STEP = 16
VMEM_BYTES = 50 * 1024 * 1024
F32 = jnp.float32
BF16 = jnp.bfloat16


def column_info(pair_values, columns):
    boundary = M - pair_values[:, None]
    first_part = columns[None, :] < boundary
    valid_cols = columns[None, :] < M + 1
    second_part = jnp.logical_and(valid_cols, jnp.logical_not(first_part))
    offset = jnp.where(first_part, columns[None, :], columns[None, :] - boundary)
    parity = (1 - 2 * (offset % 2)).astype(jnp.float32)
    degree = jnp.where(first_part, pair_values[:, None] + columns[None, :], columns[None, :] - 1)
    return (
        first_part.astype(jnp.float32),
        second_part.astype(jnp.float32),
        parity,
        degree.astype(jnp.float32),
    )


def wave_numbers(pair_values):
    return jnp.stack([pair_values, M - 1 - pair_values], axis=-1)


def angles(wave_table, positions, length):
    winding = wave_table[..., None] * positions % length
    return winding.astype(jnp.float32) * (2.0 * math.pi / length)


def plain_body(spec, legendre, wave_pairs, row_waves, forcing, helm_coef):
    groups = lax.axis_size("lat")
    lat_id = lax.axis_index("lat")
    lon_id = lax.axis_index("lon")
    fields, _, slot_count, col_width = spec.shape
    half_lats = legendre.shape[2]
    lats_total = 2 * half_lats
    band_rows = row_waves.shape[0]
    seg_width = forcing.shape[2]
    lons_total = seg_width * lax.axis_size("lon")
    my_pairs = lax.dynamic_slice_in_dim(wave_pairs, lat_id * slot_count, slot_count)
    columns = lon_id * col_width + jnp.arange(col_width, dtype=jnp.int32)
    first_part, second_part, parity, degree = column_info(my_pairs, columns)
    selector = jnp.stack([first_part, second_part])
    flip_signs = jnp.stack([jnp.ones_like(parity), parity])
    factor = (selector[:, None] * flip_signs[None]).astype(jnp.bfloat16)
    mixed_terms = factor[:, :, None, None] * spec.astype(jnp.bfloat16)[None, None]
    upward = jnp.einsum(
        "qhfrsc,sck->hkfrsq", mixed_terms, legendre, preferred_element_type=jnp.float32
    ) * (0.5 / math.sqrt(M))
    lat_rows = jnp.concatenate([upward[0], jnp.flip(upward[1], axis=0)], axis=0)
    partial_value = lat_rows.reshape(lats_total, -1).astype(jnp.bfloat16)
    wave_table = wave_numbers(wave_pairs).reshape(groups, slot_count * 2)
    kept_mask = (wave_table[None, :, None, None, :] < row_waves[:, None, None, None, None]).astype(
        jnp.float32
    )
    shares = lax.psum_scatter(
        partial_value.astype(jnp.float32).astype(jnp.bfloat16),
        "lon",
        scatter_dimension=1,
        tiled=True,
    )
    banded = lax.all_to_all(shares, "lat", split_axis=0, concat_axis=1, tiled=True)
    whole = lax.all_gather(banded.reshape(band_rows, groups, -1), "lon", axis=2, tiled=True)
    fourier = whole.reshape(band_rows, groups, fields, 2, slot_count * 2) * kept_mask.astype(
        jnp.bfloat16
    )
    places = lon_id * seg_width + jnp.arange(seg_width, dtype=jnp.int32)
    phases = angles(wave_table, places, lons_total)
    weight = jnp.where(wave_table == 0, 1.0, 2.0).astype(jnp.float32)[..., None]
    forward_table = jnp.stack([weight * jnp.cos(phases), -weight * jnp.sin(phases)]).astype(
        jnp.bfloat16
    )
    grid_field = jnp.einsum(
        "lgfrn,rgnx->flx", fourier, forward_table, preferred_element_type=jnp.float32
    )
    tendency = (forcing - 0.5 * grid_field * grid_field).astype(jnp.bfloat16)
    back_table = (jnp.stack([jnp.cos(phases), -jnp.sin(phases)]) / lons_total).astype(jnp.bfloat16)
    pieces = jnp.einsum("flx,rgnx->lgfrn", tendency, back_table, preferred_element_type=jnp.float32)
    pieces = (pieces * kept_mask).astype(jnp.bfloat16)
    shares_back = lax.psum_scatter(
        pieces.reshape(band_rows, groups, -1).astype(jnp.float32).astype(jnp.bfloat16),
        "lon",
        scatter_dimension=2,
        tiled=True,
    )
    swapped = lax.all_to_all(shares_back, "lat", split_axis=1, concat_axis=0, tiled=True)
    fan_flat = lax.all_gather(swapped, "lon", axis=2, tiled=True).reshape(lats_total, -1)
    fan_rows = fan_flat.reshape(lats_total, fields, 2, slot_count, 2)
    mixed_back = jnp.stack([fan_rows[:half_lats], jnp.flip(fan_rows[half_lats:], axis=0)])
    downward = jnp.einsum(
        "hkfrsq,sck->frsqhc", mixed_back, legendre, preferred_element_type=jnp.float32
    )
    spectral_tendency = (
        first_part * (downward[:, :, :, 0, 0] + parity * downward[:, :, :, 0, 1])
        + second_part * (downward[:, :, :, 1, 0] + parity * downward[:, :, :, 1, 1])
    ) * math.sqrt(M)
    valid_cols = first_part + second_part
    divisor = 1.0 + helm_coef[:, None, None, None] * (degree * (degree + 1.0))[None, None]
    spec_new = valid_cols[None, None] * (spec + spectral_tendency) / divisor
    return (grid_field, spec_new)


SOURCES = (0, 4, 2, 6, 1, 5, 3, 7)
STEPS = (0, 1, 0, 2, 0, 1, 2, 1, None, 0, 2, 1, 0, 1, 2, 0, 2, 1, 0, 1, 3, 4, 0, 2, 0, 1, 2, 1, 5, 2, 0, 2, 1, 2)


def row_of(h, q, d, r):
    return ((h * 2 + q) * 4 + d) * 2 + r


def dot(a, b):
    return jnp.dot(a, b, preferred_element_type=F32)


def dot_nt(a, b):
    return lax.dot_general(a, b, (((1,), (1,)), ((), ())), preferred_element_type=F32)


def low_half():
    return lax.broadcasted_iota(jnp.int32, (STEP, LANES), 1) < HALF


def tile_groups(tiles, packed, groups):
    if packed:
        return [(n, 2 * n) for n in range(len(tiles))]
    return [(n, n) for n in range(len(tiles))]


def up_kernel(place, mix, *refs, tiles, packed, groups, scale):
    legs, (keep, send, scratch) = refs[: len(tiles)], refs[len(tiles) :]
    me = place[0]
    rows = mix.shape[1]
    for s in range(STEP):
        basis = jnp.concatenate([leg[s] for leg in legs], axis=1)
        found = dot(mix[s], basis) * scale
        for n in range(len(tiles)):
            scratch[n, s * rows : (s + 1) * rows, :] = found[:, n * LANES : (n + 1) * LANES]

    def fetch(h, q, d, r, n):
        return scratch[n, pl.ds(row_of(h, q, d, r), STEP, stride=rows), :]

    for h in range(2):
        for q in range(2):
            for d in range(4):
                target = (keep, send)[d % 2]
                for n, group in tile_groups(tiles, packed, groups):
                    slot = me ^ (groups - 1 - group if h else group)
                    if packed:
                        real, imag = fetch(h, q, d, 0, n), fetch(h, q, d, 1, n)
                        even = jnp.where(low_half(), real, pltpu.roll(imag, HALF, 1))
                        odd = jnp.where(low_half(), pltpu.roll(real, HALF, 1), imag)
                        target[d // 2, slot, q] = even.astype(BF16)
                        target[d // 2, slot ^ 1, q] = odd.astype(BF16)
                    else:
                        for r in range(2):
                            target[d // 2, slot, r, q] = fetch(h, q, d, r, n).astype(BF16)


def up_chunk(place, mix, legendre, tiles, packed, groups, scale):
    slots, rows, width = mix.shape
    lead = (2, groups, 2) if packed else (2, groups, 2, 2)
    out = jax.ShapeDtypeStruct(lead + (slots, LANES), BF16)
    out_spec = pl.BlockSpec(lead + (STEP, LANES), lambda i, p: (0,) * len(lead) + (i, 0))

    def leg_spec(tile):
        return pl.BlockSpec((STEP, width, LANES), lambda i, p: (i, 0, tile))

    return pl.pallas_call(
        lambda *refs: up_kernel(*refs, tiles=tiles, packed=packed, groups=groups, scale=scale),
        out_shape=(out, out),
        grid_spec=pltpu.PrefetchScalarGridSpec(
            num_scalar_prefetch=1,
            grid=(slots // STEP,),
            in_specs=[pl.BlockSpec((STEP, rows, width), lambda i, p: (i, 0, 0))]
            + [leg_spec(t) for t in tiles],
            out_specs=(out_spec, out_spec),
            scratch_shapes=[pltpu.VMEM((len(tiles), STEP * rows, LANES), F32)],
        ),
        compiler_params=pltpu.CompilerParams(vmem_limit_bytes=VMEM_BYTES),
        cost_estimate=pl.CostEstimate(
            flops=2 * slots * 256 * 2 * width * len(tiles) * LANES // 2,
            bytes_accessed=slots * width * len(tiles) * LANES * 2,
            transcendentals=0,
        ),
        name="legendre_up",
    )(place, mix, *[legendre] * len(tiles))


def down_kernel(place, *refs, tiles, packed, groups, first, last):
    fans, legs = refs[:4], refs[4 : 4 + len(tiles)]
    rest = list(refs[4 + len(tiles) :])
    factors = rest.pop(0)
    previous = None if first else rest.pop(0)
    spec, inverse = (rest.pop(0), rest.pop(0)) if last else (None, None)
    out, scratch, sums = rest
    me, mine = place[0], place[1]
    rows = 32

    def put(h, q, d, r, n, value):
        scratch[n, pl.ds(row_of(h, q, d, r), STEP, stride=rows), :] = value

    for h in range(2):
        for q in range(2):
            for d in range(4):
                for n, group in tile_groups(tiles, packed, groups):
                    slot = me ^ (groups - 1 - group if h else group)
                    if packed:
                        even = fans[d][slot, q].astype(F32)
                        odd = fans[d][slot ^ 1, q].astype(F32)
                        put(h, q, d, 0, n, jnp.where(low_half(), even, pltpu.roll(odd, HALF, 1)))
                        put(h, q, d, 1, n, jnp.where(low_half(), pltpu.roll(even, HALF, 1), odd))
                    else:
                        for r in range(2):
                            put(h, q, d, r, n, fans[d][slot, r, q].astype(F32))
    for s in range(STEP):
        basis = jnp.concatenate([leg[s] for leg in legs], axis=1)
        values = [scratch[n, s * rows : (s + 1) * rows, :] for n in range(len(tiles))]
        values = jnp.concatenate(values, axis=1).astype(BF16)
        found = dot_nt(values, basis)
        total = sum(found[8 * n : 8 * n + 8] * factors[s, n : n + 1, :] for n in range(4))
        for n in range(8):
            sums[n, s : s + 1, :] = total[n : n + 1]
    for d in range(4):
        field = mine ^ d
        for r in range(2):
            n = 2 * d + r
            total = sums[n]
            if not first:
                total = total + previous[field, r]
            if last:
                total = (spec[field, r] + total * math.sqrt(M)) * inverse[field]
            out[field, r] = total


def down_chunk(place, fans, legendre, factors, previous, spec, inverse, tiles, packed, groups):
    slots, _, width = factors.shape
    first, last = previous is None, spec is not None
    lead = (groups, 2) if packed else (groups, 2, 2)
    fan_spec = pl.BlockSpec(lead + (STEP, LANES), lambda i, p: (0,) * len(lead) + (i, 0))
    field_spec = pl.BlockSpec((4, 2, STEP, width), lambda i, p: (0, 0, i, 0))

    def leg_spec(tile):
        return pl.BlockSpec((STEP, width, LANES), lambda i, p: (i, 0, tile))

    operands = [*fans, *[legendre] * len(tiles), factors]
    specs = [fan_spec] * 4 + [leg_spec(t) for t in tiles]
    specs.append(pl.BlockSpec((STEP, 4, width), lambda i, p: (i, 0, 0)))
    if not first:
        operands.append(previous)
        specs.append(field_spec)
    if last:
        operands += [spec, inverse]
        specs += [field_spec, pl.BlockSpec((4, STEP, width), lambda i, p: (0, i, 0))]
    return pl.pallas_call(
        lambda *refs: down_kernel(
            *refs, tiles=tiles, packed=packed, groups=groups, first=first, last=last
        ),
        out_shape=jax.ShapeDtypeStruct((4, 2, slots, width), F32),
        grid_spec=pltpu.PrefetchScalarGridSpec(
            num_scalar_prefetch=1,
            grid=(slots // STEP,),
            in_specs=specs,
            out_specs=field_spec,
            scratch_shapes=[
                pltpu.VMEM((len(tiles), STEP * 32, LANES), F32),
                pltpu.VMEM((8, STEP, width), F32),
            ],
        ),
        compiler_params=pltpu.CompilerParams(vmem_limit_bytes=VMEM_BYTES),
        cost_estimate=pl.CostEstimate(
            flops=2 * slots * 256 * width * len(tiles) * LANES,
            bytes_accessed=slots * width * len(tiles) * LANES * 2,
            transcendentals=0,
        ),
        name="legendre_down",
    )(place, *operands)


def table_kernel(cos_far, sin_far, cos_near, sin_near, out):
    for n in range(cos_far.shape[1]):
        lanes = slice(n * LANES, (n + 1) * LANES)
        cos_a, sin_a = cos_far[:, n : n + 1], sin_far[:, n : n + 1]
        cos_b, sin_b = cos_near[...], sin_near[...]
        out[0, 0, :, lanes] = (cos_a * cos_b - sin_a * sin_b).astype(BF16)
        out[1, 0, :, lanes] = (-sin_a * cos_b - cos_a * sin_b).astype(BF16)


def make_table(waves, first_place, width, length, groups):
    far = angles(waves, first_place + LANES * jnp.arange(width // LANES, dtype=jnp.int32), length)
    near = angles(waves, jnp.arange(LANES, dtype=jnp.int32), length)
    count = waves.shape[0] // groups
    far_spec = pl.BlockSpec((count, width // LANES), lambda i: (i, 0))
    near_spec = pl.BlockSpec((count, LANES), lambda i: (i, 0))
    return pl.pallas_call(
        table_kernel,
        out_shape=jax.ShapeDtypeStruct((2, groups, count, width), BF16),
        grid=(groups,),
        in_specs=[far_spec, far_spec, near_spec, near_spec],
        out_specs=pl.BlockSpec((2, 1, count, width), lambda i: (0, i, 0, 0)),
        compiler_params=pltpu.CompilerParams(vmem_limit_bytes=VMEM_BYTES),
        name="zonal_table",
    )(jnp.cos(far), jnp.sin(far), jnp.cos(near), jnp.sin(near))


def zonal_kernel(place, *refs, packed, first, groups, scale):
    blocks, rest = pieces_of([ref.at for ref in refs[:4]]), list(refs[4:])
    table, flip, spread, waves, row_waves, turns, unturns, local, f1, f2, f3 = rest[:11]
    rest = rest[11:] if first else rest[12:]
    grid, near_out, far_out, stay, leave = rest[:5]
    outs = [half.at[n] for half in (stay, leave) for n in range(groups // 2)]
    weight, values, lines, near, far, field, tend, read_sem, write_sem = rest[5:]
    mine, offset = place[1], pl.multiple_of(place[2], 16)
    far_offset = pl.multiple_of(place[3], 16)
    per_group, width = table.shape[2:]
    count = groups * per_group
    rows = HALF if packed else LANES
    block = 256
    wave_block = groups // 2

    reads = [pltpu.make_async_copy(local.at[mine, pl.ds(offset, rows), :], near, read_sem.at[0])]
    for n, ref in enumerate((f1, f2, f3)):
        reads.append(
            pltpu.make_async_copy(ref.at[pl.ds(far_offset, rows), :], far.at[n], read_sem.at[n + 1])
        )
    for read in reads:
        read.start()
    kept = waves[...] < row_waves[...]
    weight[...] = jnp.where(kept, jnp.where(waves[...] == 0, 1.0, 2.0), 0.0).astype(BF16)
    turned = []
    for r in range(2):
        for n in range(groups):
            here = slice(n * per_group, (n + 1) * per_group)
            part = blocks[n][...] if packed else blocks[n][r]
            values[here, :] = part.reshape(per_group, LANES) * weight[here, :]
        turned.append(dot_nt(flip[r] if packed else flip[...], values[...]))
    real, imag = turned
    for d in range(4):
        here = slice(d * rows, (d + 1) * rows)
        cos, sin = turns[2 * d : 2 * d + 1, :], turns[2 * d + 1 : 2 * d + 2, :]
        lines[0, here, :] = (cos * real - sin * imag).astype(BF16)
        lines[1, here, :] = (sin * real + cos * imag).astype(BF16)
    for read in reads:
        read.wait()

    @pl.loop(0, width // block)
    def _(step):
        lanes = pl.ds(pl.multiple_of(step * block, block), block)
        total = dot(lines[0], table[0, :, :, lanes].reshape(count, block))
        total += dot(lines[1], table[1, :, :, lanes].reshape(count, block))
        for d in range(4):
            here = slice(d * rows, (d + 1) * rows)
            part = total[here]
            force = far[d - 1, :, lanes].astype(F32) if d else near[:, lanes]
            if d == 0:
                field[:, lanes] = part
            elif d == 1:
                near_out[:, lanes] = part.astype(BF16)
            else:
                far_out[d - 2, :, lanes] = part.astype(BF16)
            tend[here, lanes] = (force - 0.5 * part * part).astype(BF16)

    write = pltpu.make_async_copy(field, grid.at[mine, pl.ds(offset, rows), :], write_sem)
    write.start()
    some = wave_block * per_group
    for step in range(groups // wave_block):
        several = slice(step * wave_block, (step + 1) * wave_block)
        here = slice(step * some, (step + 1) * some)
        mask = weight[here, :].astype(F32) > 0
        real = dot_nt(table[0, several].reshape(some, width), tend[...])
        imag = dot_nt(table[1, several].reshape(some, width), tend[...])
        sum_real, sum_imag = 0.0, 0.0
        for n in range(4 * rows // LANES):
            lanes = slice(n * LANES, (n + 1) * LANES)
            if packed:
                low = lax.broadcasted_iota(jnp.int32, (some, LANES), 1) < HALF
                cos = jnp.where(low, unturns[here, 4 * n : 4 * n + 1], unturns[here, 4 * n + 2 : 4 * n + 3])
                sin = jnp.where(low, unturns[here, 4 * n + 1 : 4 * n + 2], unturns[here, 4 * n + 3 : 4 * n + 4])
            else:
                cos, sin = unturns[here, 2 * n : 2 * n + 1], unturns[here, 2 * n + 1 : 2 * n + 2]
            sum_real += cos * real[:, lanes] + sin * imag[:, lanes]
            sum_imag += cos * imag[:, lanes] - sin * real[:, lanes]
        sums = [(v * scale).astype(BF16) for v in (sum_real, sum_imag)]
        if packed:
            parts = [dot(sums[0], spread[0]) + dot(sums[1], spread[1])]
        else:
            parts = [dot(v, flip[...]) for v in sums]
        for r, part in enumerate(parts):
            part = jnp.where(mask, part, 0.0).astype(BF16)
            for n in range(wave_block):
                out = outs[step * wave_block + n]
                piece = part[n * per_group : (n + 1) * per_group]
                if packed:
                    out[...] = piece.reshape(out.shape)
                else:
                    out[r] = piece.reshape(out.shape[1:])
    write.wait()


def zonal_chunk(place, arrays, table, setup, waves, turns, forcing, far_forcing, grid, packed, scale):
    flip, spread, row_waves = setup
    _, groups, per_group, width = table.shape
    count = groups * per_group
    rows = HALF if packed else LANES
    first = grid is None
    half = jax.ShapeDtypeStruct(arrays[0].shape, BF16)
    vmem, anywhere = pl.BlockSpec(memory_space=pltpu.VMEM), pl.BlockSpec(memory_space=pl.ANY)
    operands = [place, *arrays, table, flip, spread, waves, row_waves, turns, turns.T, forcing, *far_forcing]
    specs = [pl.BlockSpec(memory_space=pltpu.SMEM)] + [vmem] * 11 + [anywhere] * 4
    aliases = {}
    if not first:
        aliases = {len(operands): 0}
        operands.append(grid)
        specs.append(anywhere)
    grid, near, far, stay, leave = pl.pallas_call(
        lambda *refs: zonal_kernel(*refs, packed=packed, first=first, groups=groups, scale=scale),
        out_shape=(
            jax.ShapeDtypeStruct(forcing.shape, F32),
            jax.ShapeDtypeStruct((rows, width), BF16),
            jax.ShapeDtypeStruct((2, rows, width), BF16),
            half,
            half,
        ),
        in_specs=specs,
        out_specs=(anywhere, vmem, vmem, vmem, vmem),
        scratch_shapes=[
            pltpu.VMEM((count, LANES), BF16),
            pltpu.VMEM((count, LANES), BF16),
            pltpu.VMEM((2, 4 * rows, count), BF16),
            pltpu.VMEM((rows, width), F32),
            pltpu.VMEM((3, rows, width), BF16),
            pltpu.VMEM((rows, width), F32),
            pltpu.VMEM((4 * rows, width), BF16),
            pltpu.SemaphoreType.DMA((4,)),
            pltpu.SemaphoreType.DMA,
        ],
        input_output_aliases=aliases,
        compiler_params=pltpu.CompilerParams(vmem_limit_bytes=VMEM_BYTES),
        cost_estimate=pl.CostEstimate(
            flops=2 * 2 * 2 * 4 * rows * count * width,
            bytes_accessed=2 * 2 * count * width + 2 * 4 * 4 * rows * width,
            transcendentals=0,
        ),
        name="zonal",
    )(*operands)
    return grid, near, far, stay, leave


def settle_kernel(place, g1, g2, g3, before, grid, wide, sem):
    mine, offset = place[1], pl.multiple_of(place[2], 8)
    rows = g1.shape[0]
    copies = []
    for n, ref in enumerate((g1, g2, g3)):
        wide[n] = ref[...].astype(F32)
        target = grid.at[mine ^ (n + 1), pl.ds(offset, rows), :]
        copies.append(pltpu.make_async_copy(wide.at[n], target, sem.at[n]))
        copies[-1].start()
    for copy in copies:
        copy.wait()


def settle(place, pieces, grid):
    vmem, anywhere = pl.BlockSpec(memory_space=pltpu.VMEM), pl.BlockSpec(memory_space=pl.ANY)
    return pl.pallas_call(
        settle_kernel,
        out_shape=jax.ShapeDtypeStruct(grid.shape, F32),
        in_specs=[pl.BlockSpec(memory_space=pltpu.SMEM), vmem, vmem, vmem, anywhere],
        out_specs=anywhere,
        scratch_shapes=[pltpu.VMEM((3,) + pieces[0].shape, F32), pltpu.SemaphoreType.DMA((3,))],
        input_output_aliases={4: 0},
        compiler_params=pltpu.CompilerParams(vmem_limit_bytes=VMEM_BYTES),
        name="settle",
    )(place, *pieces, grid)


def swap(value, axis, bit):
    pairs = [(n, n ^ bit) for n in range(lax.axis_size(axis))]
    return lax.ppermute(value, axis, pairs)


def add(*values):
    return sum(v.astype(F32) for v in values).astype(BF16)


def spread_lon(near, far):
    arrived = swap(far, "lon", 2)
    return swap(near, "lon", 1), arrived[0], swap(arrived[1], "lon", 1)


def pieces_of(arrays):
    kept, one, two, three = arrays
    return [kept[0], one[0], two[0], two[2], three[0], three[1], three[2], three[3]]


class Turns:
    def __init__(self):
        self.last = None

    def run(self, step, *inputs):
        if self.last is not None:
            inputs, _ = lax.optimization_barrier((inputs, self.last))
        found = step(*inputs)
        self.last = jax.tree.leaves(found)[-1]
        return found


def exchange_lat(run, stay, leave, bits):
    one = swap(leave, "lat", bits[0])
    yield
    two = swap(run(lambda s, a: jnp.concatenate([s[2:], a[2:]]), stay, one), "lat", bits[1])
    yield
    leave = run(lambda s, a, b: jnp.stack([s[1], a[1], b[1], b[3]]), stay, one, two)
    three = swap(leave, "lat", bits[2])
    return stay, one, two, three


def fast_plan(spec, legendre, row_waves, forcing):
    groups, lon_size = lax.axis_size("lat"), lax.axis_size("lon")
    fields, _, slots, _ = spec.shape
    half_lats, band, width = legendre.shape[2], row_waves.shape[0], forcing.shape[2]
    per_pair, odd = divmod(2 * band, LANES)
    if (groups, lon_size, fields) != (8, 4, 4) or odd or per_pair != 5:
        return None
    if slots % STEP or half_lats != 4 * band or width % 256 or 2 * slots % STEP:
        return None
    pairs = range(half_lats // (2 * band))
    full = [
        [t for p in pairs for t in (per_pair * p + n, per_pair * (p + 1) - 1 - n)]
        for n in range(per_pair // 2)
    ]
    return [per_pair * p + per_pair // 2 for p in pairs], full


def body(spec, legendre, wave_pairs, row_waves, forcing, helm_coef):
    plan = fast_plan(spec, legendre, row_waves, forcing)
    if plan is None:
        return plain_body(spec, legendre, wave_pairs, row_waves, forcing, helm_coef)
    shared_tiles, full_tiles = plan
    groups = lax.axis_size("lat")
    lat_id, lon_id = lax.axis_index("lat"), lax.axis_index("lon")
    fields, _, slots, col_width = spec.shape
    band, seg_width = row_waves.shape[0], forcing.shape[2]
    length = seg_width * lax.axis_size("lon")
    top = groups // 2

    my_pairs = lax.dynamic_slice_in_dim(wave_pairs, lat_id * slots, slots)
    columns = lon_id * col_width + jnp.arange(col_width, dtype=jnp.int32)
    first_part, second_part, parity, degree = column_info(my_pairs, columns)
    factors = jnp.stack(
        [first_part, second_part, parity * first_part, parity * second_part], axis=1
    )
    near = jnp.stack([lax.dynamic_index_in_dim(spec, lon_id ^ d, 0, False) for d in range(4)])
    near = jnp.transpose(near.astype(BF16), (2, 0, 1, 3)).reshape(slots, 1, 2 * fields, col_width)
    mix = (factors[:, :, None].astype(BF16) * near).reshape(slots, 8 * fields, col_width)
    divisor = 1.0 + helm_coef[:, None, None] * (degree * (degree + 1.0))[None]
    inverse = (first_part + second_part)[None] / divisor

    grouped = wave_pairs.reshape(groups, slots)
    near_pairs = jnp.stack(
        [lax.dynamic_index_in_dim(grouped, lat_id ^ e, 0, False) for e in SOURCES]
    )
    waves = jnp.stack([near_pairs, M - 1 - near_pairs], axis=1).reshape(-1)
    quarter = waves[None] * (lon_id ^ jnp.arange(4, dtype=jnp.int32))[:, None] % 4
    cosine = jnp.where(quarter == 0, 1, jnp.where(quarter == 2, -1, 0))
    sine = jnp.where(quarter == 1, 1, jnp.where(quarter == 3, -1, 0))
    turns = jnp.stack([cosine, sine], axis=1).reshape(8, -1).astype(F32)

    south = lat_id >= top
    north = jnp.where(south, groups - 1 - lat_id, lat_id)
    row = jnp.arange(LANES, dtype=jnp.int32)
    place = jnp.stack([lat_id, lon_id])
    chunks = [(full_tiles[0], False, 0), (shared_tiles, True, 0), (full_tiles[1], False, 1)]
    setups, starts = [], []
    for tiles, packed, n in chunks:
        rows = HALF if packed else LANES
        start = band - rows if packed else n * LANES
        start = jnp.where(north % 2 == 0, start, band - rows - start)
        start = jnp.where(south, band - rows - start, start)
        mirrored = jnp.where(south, rows - 1 - row[:rows], row[:rows])
        if packed:
            target = HALF * jnp.arange(2)[:, None] + mirrored[None]
            flip = target[..., None] == row
            spread = jnp.concatenate([flip, flip], axis=1).astype(BF16)
        else:
            flip = mirrored[:, None] == row
            spread = jnp.zeros((8, LANES), BF16)
        kept = lax.dynamic_slice_in_dim(row_waves, start, rows)
        kept = jnp.sum(jnp.where(flip, kept[:, None], 0), axis=tuple(range(flip.ndim - 1)))
        starts.append(start)
        setups.append(((flip.astype(BF16), spread, kept[None].astype(jnp.int32))))

    def far_rows(forcing, start, rows):
        near, *far = [
            lax.dynamic_slice(forcing, (lon_id ^ d, start, 0), (1, rows, seg_width))[0].astype(BF16)
            for d in (1, 2, 3)
        ]
        return near, jnp.stack(far)

    split = [LANES, band - LANES]
    after_first = jnp.where(starts[0] == 0, LANES, 0)
    offsets = [jnp.zeros_like(starts[0])] + [s - after_first for s in starts[1:]]
    spots = [
        jnp.stack([lat_id, lon_id, s, o]).astype(jnp.int32) for s, o in zip(starts, offsets)
    ]
    turn = Turns()
    run = turn.run
    first_force = spread_lon(*run(lambda f: far_rows(f, starts[0], split[0]), forcing))
    state = {"grid": None, "total": None, "force": None, "table": None}

    def chunk_steps(n):
        tiles, packed, _ = chunks[n]
        keep, send = run(
            lambda p, m, l: up_chunk(p, m, l, tiles, packed, groups, 0.5 / math.sqrt(M)), place, mix, legendre
        )
        yield
        other_far, other_own = swap(send[1], "lon", 1), swap(send[0], "lon", 1)
        away = swap(run(lambda k, o: add(k[1], o), keep, other_far), "lon", 2)
        if n == 2:
            state["force"] = spread_lon(*run(lambda f: far_rows(f, after_first, split[1]), forcing))
        yield
        half = groups // 2
        stay, leave = run(
            lambda k, o, a: (add(k[0, :half], o[:half], a[:half]), add(k[0, half:], o[half:], a[half:])),
            keep, other_own, away,
        )
        arrays = yield from exchange_lat(run, stay, leave, (4, 2, 1))
        yield
        force = state["force"] if n else first_force
        grid, near, far, stay, leave = run(
            lambda *a: zonal_chunk(
                spots[n], a[:4], a[4], setups[n], waves[:, None], turns, forcing, a[5:], state["grid"], packed, 1.0 / length
            ),
            *arrays, state["table"], *force,
        )
        state["grid"] = grid
        settled.append((spots[n], spread_lon(near, far)))
        arrays = yield from exchange_lat(run, stay, leave, (1, 2, 4))
        yield
        own = run(lambda *a: jnp.stack(pieces_of(a)), *arrays)
        across = swap(own, "lon", 2)
        fans = own, swap(own, "lon", 1), across, swap(across, "lon", 1)
        yield
        state["total"] = run(
            lambda *a: down_chunk(
                place, a, legendre, factors, state["total"], spec if n == 2 else None,
                inverse if n == 2 else None, tiles, packed, groups,
            ),
            *fans,
        )
        yield

    settled = []
    walks = [chunk_steps(n) for n in range(3)]
    for step in STEPS:
        if step is None:
            state["table"] = run(lambda w: make_table(w, 0, seg_width, length, groups), waves)
        elif step < 3:
            next(walks[step])
        else:
            spot, parts = settled[step - 3]
            state["grid"] = run(lambda *a: settle(spot, a, state["grid"]), *parts)
    return state["grid"], state["total"]


def solution(mesh):
    return jax.shard_map(
        body,
        mesh=mesh,
        in_specs=(
            P(None, None, "lat", "lon"),
            P("lat", "lon", None),
            P(),
            P("lat"),
            P(None, "lat", "lon"),
            P(),
        ),
        out_specs=(P(None, "lat", "lon"), P(None, None, "lat", "lon")),
        check_vma=False,
    )
```

```python
import math

import jax
import jax.numpy as jnp
from jax import lax
from jax.experimental import pallas as pl
from jax.experimental.pallas import tpu as pltpu
from jax.sharding import PartitionSpec as P

M = 1280
LANES = 128
HALF = LANES // 2
STEP = 16
VMEM_BYTES = 50 * 1024 * 1024
F32 = jnp.float32
BF16 = jnp.bfloat16


def column_info(pair_values, columns):
    boundary = M - pair_values[:, None]
    first_part = columns[None, :] < boundary
    valid_cols = columns[None, :] < M + 1
    second_part = jnp.logical_and(valid_cols, jnp.logical_not(first_part))
    offset = jnp.where(first_part, columns[None, :], columns[None, :] - boundary)
    parity = (1 - 2 * (offset % 2)).astype(jnp.float32)
    degree = jnp.where(first_part, pair_values[:, None] + columns[None, :], columns[None, :] - 1)
    return (
        first_part.astype(jnp.float32),
        second_part.astype(jnp.float32),
        parity,
        degree.astype(jnp.float32),
    )


def wave_numbers(pair_values):
    return jnp.stack([pair_values, M - 1 - pair_values], axis=-1)


def angles(wave_table, positions, length):
    winding = wave_table[..., None] * positions % length
    return winding.astype(jnp.float32) * (2.0 * math.pi / length)


def plain_body(spec, legendre, wave_pairs, row_waves, forcing, helm_coef):
    groups = lax.axis_size("lat")
    lat_id = lax.axis_index("lat")
    lon_id = lax.axis_index("lon")
    fields, _, slot_count, col_width = spec.shape
    half_lats = legendre.shape[2]
    lats_total = 2 * half_lats
    band_rows = row_waves.shape[0]
    seg_width = forcing.shape[2]
    lons_total = seg_width * lax.axis_size("lon")
    my_pairs = lax.dynamic_slice_in_dim(wave_pairs, lat_id * slot_count, slot_count)
    columns = lon_id * col_width + jnp.arange(col_width, dtype=jnp.int32)
    first_part, second_part, parity, degree = column_info(my_pairs, columns)
    selector = jnp.stack([first_part, second_part])
    flip_signs = jnp.stack([jnp.ones_like(parity), parity])
    factor = (selector[:, None] * flip_signs[None]).astype(jnp.bfloat16)
    mixed_terms = factor[:, :, None, None] * spec.astype(jnp.bfloat16)[None, None]
    upward = jnp.einsum(
        "qhfrsc,sck->hkfrsq", mixed_terms, legendre, preferred_element_type=jnp.float32
    ) * (0.5 / math.sqrt(M))
    lat_rows = jnp.concatenate([upward[0], jnp.flip(upward[1], axis=0)], axis=0)
    partial_value = lat_rows.reshape(lats_total, -1).astype(jnp.bfloat16)
    wave_table = wave_numbers(wave_pairs).reshape(groups, slot_count * 2)
    kept_mask = (wave_table[None, :, None, None, :] < row_waves[:, None, None, None, None]).astype(
        jnp.float32
    )
    shares = lax.psum_scatter(
        partial_value.astype(jnp.float32).astype(jnp.bfloat16),
        "lon",
        scatter_dimension=1,
        tiled=True,
    )
    banded = lax.all_to_all(shares, "lat", split_axis=0, concat_axis=1, tiled=True)
    whole = lax.all_gather(banded.reshape(band_rows, groups, -1), "lon", axis=2, tiled=True)
    fourier = whole.reshape(band_rows, groups, fields, 2, slot_count * 2) * kept_mask.astype(
        jnp.bfloat16
    )
    places = lon_id * seg_width + jnp.arange(seg_width, dtype=jnp.int32)
    phases = angles(wave_table, places, lons_total)
    weight = jnp.where(wave_table == 0, 1.0, 2.0).astype(jnp.float32)[..., None]
    forward_table = jnp.stack([weight * jnp.cos(phases), -weight * jnp.sin(phases)]).astype(
        jnp.bfloat16
    )
    grid_field = jnp.einsum(
        "lgfrn,rgnx->flx", fourier, forward_table, preferred_element_type=jnp.float32
    )
    tendency = (forcing - 0.5 * grid_field * grid_field).astype(jnp.bfloat16)
    back_table = (jnp.stack([jnp.cos(phases), -jnp.sin(phases)]) / lons_total).astype(jnp.bfloat16)
    pieces = jnp.einsum("flx,rgnx->lgfrn", tendency, back_table, preferred_element_type=jnp.float32)
    pieces = (pieces * kept_mask).astype(jnp.bfloat16)
    shares_back = lax.psum_scatter(
        pieces.reshape(band_rows, groups, -1).astype(jnp.float32).astype(jnp.bfloat16),
        "lon",
        scatter_dimension=2,
        tiled=True,
    )
    swapped = lax.all_to_all(shares_back, "lat", split_axis=1, concat_axis=0, tiled=True)
    fan_flat = lax.all_gather(swapped, "lon", axis=2, tiled=True).reshape(lats_total, -1)
    fan_rows = fan_flat.reshape(lats_total, fields, 2, slot_count, 2)
    mixed_back = jnp.stack([fan_rows[:half_lats], jnp.flip(fan_rows[half_lats:], axis=0)])
    downward = jnp.einsum(
        "hkfrsq,sck->frsqhc", mixed_back, legendre, preferred_element_type=jnp.float32
    )
    spectral_tendency = (
        first_part * (downward[:, :, :, 0, 0] + parity * downward[:, :, :, 0, 1])
        + second_part * (downward[:, :, :, 1, 0] + parity * downward[:, :, :, 1, 1])
    ) * math.sqrt(M)
    valid_cols = first_part + second_part
    divisor = 1.0 + helm_coef[:, None, None, None] * (degree * (degree + 1.0))[None, None]
    spec_new = valid_cols[None, None] * (spec + spectral_tendency) / divisor
    return (grid_field, spec_new)


SOURCES = (0, 4, 2, 6, 1, 5, 3, 7)
STEPS = (0, 1, 0, 2, 0, 1, 2, 1, None, 0, 2, 1, "force", 0, 1, 2, 0, 2, 1, 0, 1, 3, 4, 0, 2, 0, 1, 2, 1, 2, 0, 2, "grid", 1, 2, 5)


def row_of(h, q, d, r):
    return ((h * 2 + q) * 4 + d) * 2 + r


def dot(a, b):
    return jnp.dot(a, b, preferred_element_type=F32)


def dot_nt(a, b):
    return lax.dot_general(a, b, (((1,), (1,)), ((), ())), preferred_element_type=F32)


def low_half():
    return lax.broadcasted_iota(jnp.int32, (STEP, LANES), 1) < HALF


def tile_groups(tiles, packed, groups):
    if packed:
        return [(n, 2 * n) for n in range(len(tiles))]
    return [(n, n) for n in range(len(tiles))]


def up_kernel(place, mix, *refs, tiles, packed, groups, scale):
    legs, (keep, send, scratch) = refs[: len(tiles)], refs[len(tiles) :]
    me = place[0]
    rows = mix.shape[1]
    for s in range(STEP):
        basis = jnp.concatenate([leg[s] for leg in legs], axis=1)
        found = dot(mix[s], basis) * scale
        for n in range(len(tiles)):
            scratch[n, s * rows : (s + 1) * rows, :] = found[:, n * LANES : (n + 1) * LANES]

    def fetch(h, q, d, r, n):
        return scratch[n, pl.ds(row_of(h, q, d, r), STEP, stride=rows), :]

    for h in range(2):
        for q in range(2):
            for d in range(4):
                target = (keep, send)[d % 2]
                for n, group in tile_groups(tiles, packed, groups):
                    slot = me ^ (groups - 1 - group if h else group)
                    if packed:
                        real, imag = fetch(h, q, d, 0, n), fetch(h, q, d, 1, n)
                        even = jnp.where(low_half(), real, pltpu.roll(imag, HALF, 1))
                        odd = jnp.where(low_half(), pltpu.roll(real, HALF, 1), imag)
                        target[d // 2, slot, q] = even.astype(BF16)
                        target[d // 2, slot ^ 1, q] = odd.astype(BF16)
                    else:
                        for r in range(2):
                            target[d // 2, slot, r, q] = fetch(h, q, d, r, n).astype(BF16)


def up_chunk(place, mix, legendre, tiles, packed, groups, scale):
    slots, rows, width = mix.shape
    lead = (2, groups, 2) if packed else (2, groups, 2, 2)
    out = jax.ShapeDtypeStruct(lead + (slots, LANES), BF16)
    out_spec = pl.BlockSpec(lead + (STEP, LANES), lambda i, p: (0,) * len(lead) + (i, 0))

    def leg_spec(tile):
        return pl.BlockSpec((STEP, width, LANES), lambda i, p: (i, 0, tile))

    return pl.pallas_call(
        lambda *refs: up_kernel(*refs, tiles=tiles, packed=packed, groups=groups, scale=scale),
        out_shape=(out, out),
        grid_spec=pltpu.PrefetchScalarGridSpec(
            num_scalar_prefetch=1,
            grid=(slots // STEP,),
            in_specs=[pl.BlockSpec((STEP, rows, width), lambda i, p: (i, 0, 0))]
            + [leg_spec(t) for t in tiles],
            out_specs=(out_spec, out_spec),
            scratch_shapes=[pltpu.VMEM((len(tiles), STEP * rows, LANES), F32)],
        ),
        compiler_params=pltpu.CompilerParams(vmem_limit_bytes=VMEM_BYTES),
        cost_estimate=pl.CostEstimate(
            flops=2 * slots * 256 * 2 * width * len(tiles) * LANES // 2,
            bytes_accessed=slots * width * len(tiles) * LANES * 2,
            transcendentals=0,
        ),
        name="legendre_up",
    )(place, mix, *[legendre] * len(tiles))


def down_kernel(place, *refs, tiles, packed, groups, first, last):
    fans, legs = refs[:4], refs[4 : 4 + len(tiles)]
    rest = list(refs[4 + len(tiles) :])
    factors = rest.pop(0)
    previous = None if first else rest.pop(0)
    spec, inverse = (rest.pop(0), rest.pop(0)) if last else (None, None)
    out, scratch, sums = rest
    me, mine = place[0], place[1]
    rows = 32

    def put(h, q, d, r, n, value):
        scratch[n, pl.ds(row_of(h, q, d, r), STEP, stride=rows), :] = value

    for h in range(2):
        for q in range(2):
            for d in range(4):
                for n, group in tile_groups(tiles, packed, groups):
                    slot = me ^ (groups - 1 - group if h else group)
                    if packed:
                        even = fans[d][slot, q].astype(F32)
                        odd = fans[d][slot ^ 1, q].astype(F32)
                        put(h, q, d, 0, n, jnp.where(low_half(), even, pltpu.roll(odd, HALF, 1)))
                        put(h, q, d, 1, n, jnp.where(low_half(), pltpu.roll(even, HALF, 1), odd))
                    else:
                        for r in range(2):
                            put(h, q, d, r, n, fans[d][slot, r, q].astype(F32))
    for s in range(STEP):
        basis = jnp.concatenate([leg[s] for leg in legs], axis=1)
        values = [scratch[n, s * rows : (s + 1) * rows, :] for n in range(len(tiles))]
        values = jnp.concatenate(values, axis=1).astype(BF16)
        found = dot_nt(values, basis)
        total = sum(found[8 * n : 8 * n + 8] * factors[s, n : n + 1, :] for n in range(4))
        for n in range(8):
            sums[n, s : s + 1, :] = total[n : n + 1]
    for d in range(4):
        field = mine ^ d
        for r in range(2):
            n = 2 * d + r
            total = sums[n]
            if not first:
                total = total + previous[field, r]
            if last:
                total = (spec[field, r] + total * math.sqrt(M)) * inverse[field]
            out[field, r] = total


def down_chunk(place, fans, legendre, factors, previous, spec, inverse, tiles, packed, groups):
    slots, _, width = factors.shape
    first, last = previous is None, spec is not None
    lead = (groups, 2) if packed else (groups, 2, 2)
    fan_spec = pl.BlockSpec(lead + (STEP, LANES), lambda i, p: (0,) * len(lead) + (i, 0))
    field_spec = pl.BlockSpec((4, 2, STEP, width), lambda i, p: (0, 0, i, 0))

    def leg_spec(tile):
        return pl.BlockSpec((STEP, width, LANES), lambda i, p: (i, 0, tile))

    operands = [*fans, *[legendre] * len(tiles), factors]
    specs = [fan_spec] * 4 + [leg_spec(t) for t in tiles]
    specs.append(pl.BlockSpec((STEP, 4, width), lambda i, p: (i, 0, 0)))
    if not first:
        operands.append(previous)
        specs.append(field_spec)
    if last:
        operands += [spec, inverse]
        specs += [field_spec, pl.BlockSpec((4, STEP, width), lambda i, p: (0, i, 0))]
    return pl.pallas_call(
        lambda *refs: down_kernel(
            *refs, tiles=tiles, packed=packed, groups=groups, first=first, last=last
        ),
        out_shape=jax.ShapeDtypeStruct((4, 2, slots, width), F32),
        grid_spec=pltpu.PrefetchScalarGridSpec(
            num_scalar_prefetch=1,
            grid=(slots // STEP,),
            in_specs=specs,
            out_specs=field_spec,
            scratch_shapes=[
                pltpu.VMEM((len(tiles), STEP * 32, LANES), F32),
                pltpu.VMEM((8, STEP, width), F32),
            ],
        ),
        compiler_params=pltpu.CompilerParams(vmem_limit_bytes=VMEM_BYTES),
        cost_estimate=pl.CostEstimate(
            flops=2 * slots * 256 * width * len(tiles) * LANES,
            bytes_accessed=slots * width * len(tiles) * LANES * 2,
            transcendentals=0,
        ),
        name="legendre_down",
    )(place, *operands)


def table_kernel(cos_far, sin_far, cos_near, sin_near, out):
    for n in range(cos_far.shape[1]):
        lanes = slice(n * LANES, (n + 1) * LANES)
        cos_a, sin_a = cos_far[:, n : n + 1], sin_far[:, n : n + 1]
        cos_b, sin_b = cos_near[...], sin_near[...]
        out[0, 0, :, lanes] = (cos_a * cos_b - sin_a * sin_b).astype(BF16)
        out[1, 0, :, lanes] = (-sin_a * cos_b - cos_a * sin_b).astype(BF16)


def make_table(waves, first_place, width, length, groups):
    far = angles(waves, first_place + LANES * jnp.arange(width // LANES, dtype=jnp.int32), length)
    near = angles(waves, jnp.arange(LANES, dtype=jnp.int32), length)
    count = waves.shape[0] // groups
    far_spec = pl.BlockSpec((count, width // LANES), lambda i: (i, 0))
    near_spec = pl.BlockSpec((count, LANES), lambda i: (i, 0))
    return pl.pallas_call(
        table_kernel,
        out_shape=jax.ShapeDtypeStruct((2, groups, count, width), BF16),
        grid=(groups,),
        in_specs=[far_spec, far_spec, near_spec, near_spec],
        out_specs=pl.BlockSpec((2, 1, count, width), lambda i: (0, i, 0, 0)),
        compiler_params=pltpu.CompilerParams(vmem_limit_bytes=VMEM_BYTES),
        name="zonal_table",
    )(jnp.cos(far), jnp.sin(far), jnp.cos(near), jnp.sin(near))


def zonal_kernel(place, *refs, packed, first, groups, scale):
    blocks, rest = pieces_of([ref.at for ref in refs[:4]]), list(refs[4:])
    table, flip, spread, waves, row_waves, turns, unturns, local, f1, f2, f3 = rest[:11]
    rest = rest[11:] if first else rest[12:]
    grid, near_out, far_out, stay, leave = rest[:5]
    outs = [half.at[n] for half in (stay, leave) for n in range(groups // 2)]
    weight, values, lines, near, far, field, tend, read_sem, write_sem = rest[5:]
    mine, offset = place[1], pl.multiple_of(place[2], 16)
    far_offset = pl.multiple_of(place[3], 16)
    per_group, width = table.shape[2:]
    count = groups * per_group
    rows = HALF if packed else LANES
    block = 256
    wave_block = groups // 2

    reads = [pltpu.make_async_copy(local.at[mine, pl.ds(offset, rows), :], near, read_sem.at[0])]
    for n, ref in enumerate((f1, f2, f3)):
        reads.append(
            pltpu.make_async_copy(ref.at[pl.ds(far_offset, rows), :], far.at[n], read_sem.at[n + 1])
        )
    for read in reads:
        read.start()
    kept = waves[...] < row_waves[...]
    weight[...] = jnp.where(kept, jnp.where(waves[...] == 0, 1.0, 2.0), 0.0).astype(BF16)
    turned = []
    for r in range(2):
        for n in range(groups):
            here = slice(n * per_group, (n + 1) * per_group)
            part = blocks[n][...] if packed else blocks[n][r]
            values[here, :] = part.reshape(per_group, LANES) * weight[here, :]
        turned.append(dot_nt(flip[r] if packed else flip[...], values[...]))
    real, imag = turned
    for d in range(4):
        here = slice(d * rows, (d + 1) * rows)
        cos, sin = turns[2 * d : 2 * d + 1, :], turns[2 * d + 1 : 2 * d + 2, :]
        lines[0, here, :] = (cos * real - sin * imag).astype(BF16)
        lines[1, here, :] = (sin * real + cos * imag).astype(BF16)
    for read in reads:
        read.wait()

    @pl.loop(0, width // block)
    def _(step):
        lanes = pl.ds(pl.multiple_of(step * block, block), block)
        total = dot(lines[0], table[0, :, :, lanes].reshape(count, block))
        total += dot(lines[1], table[1, :, :, lanes].reshape(count, block))
        for d in range(4):
            here = slice(d * rows, (d + 1) * rows)
            part = total[here]
            force = far[d - 1, :, lanes].astype(F32) if d else near[:, lanes]
            if d == 0:
                field[:, lanes] = part
            elif d == 1:
                near_out[:, lanes] = part.astype(BF16)
            else:
                far_out[d - 2, :, lanes] = part.astype(BF16)
            tend[here, lanes] = (force - 0.5 * part * part).astype(BF16)

    write = pltpu.make_async_copy(field, grid.at[mine, pl.ds(offset, rows), :], write_sem)
    write.start()
    some = wave_block * per_group
    for step in range(groups // wave_block):
        several = slice(step * wave_block, (step + 1) * wave_block)
        here = slice(step * some, (step + 1) * some)
        mask = weight[here, :].astype(F32) > 0
        real = dot_nt(table[0, several].reshape(some, width), tend[...])
        imag = dot_nt(table[1, several].reshape(some, width), tend[...])
        sum_real, sum_imag = 0.0, 0.0
        for n in range(4 * rows // LANES):
            lanes = slice(n * LANES, (n + 1) * LANES)
            if packed:
                low = lax.broadcasted_iota(jnp.int32, (some, LANES), 1) < HALF
                cos = jnp.where(low, unturns[here, 4 * n : 4 * n + 1], unturns[here, 4 * n + 2 : 4 * n + 3])
                sin = jnp.where(low, unturns[here, 4 * n + 1 : 4 * n + 2], unturns[here, 4 * n + 3 : 4 * n + 4])
            else:
                cos, sin = unturns[here, 2 * n : 2 * n + 1], unturns[here, 2 * n + 1 : 2 * n + 2]
            sum_real += cos * real[:, lanes] + sin * imag[:, lanes]
            sum_imag += cos * imag[:, lanes] - sin * real[:, lanes]
        sums = [(v * scale).astype(BF16) for v in (sum_real, sum_imag)]
        if packed:
            parts = [dot(sums[0], spread[0]) + dot(sums[1], spread[1])]
        else:
            parts = [dot(v, flip[...]) for v in sums]
        for r, part in enumerate(parts):
            part = jnp.where(mask, part, 0.0).astype(BF16)
            for n in range(wave_block):
                out = outs[step * wave_block + n]
                piece = part[n * per_group : (n + 1) * per_group]
                if packed:
                    out[...] = piece.reshape(out.shape)
                else:
                    out[r] = piece.reshape(out.shape[1:])
    write.wait()


def zonal_chunk(place, arrays, table, setup, waves, turns, forcing, far_forcing, grid, packed, scale):
    flip, spread, row_waves = setup
    _, groups, per_group, width = table.shape
    count = groups * per_group
    rows = HALF if packed else LANES
    first = grid is None
    half = jax.ShapeDtypeStruct(arrays[0].shape, BF16)
    vmem, anywhere = pl.BlockSpec(memory_space=pltpu.VMEM), pl.BlockSpec(memory_space=pl.ANY)
    operands = [place, *arrays, table, flip, spread, waves, row_waves, turns, turns.T, forcing, *far_forcing]
    specs = [pl.BlockSpec(memory_space=pltpu.SMEM)] + [vmem] * 11 + [anywhere] * 4
    aliases = {}
    if not first:
        aliases = {len(operands): 0}
        operands.append(grid)
        specs.append(anywhere)
    grid, near, far, stay, leave = pl.pallas_call(
        lambda *refs: zonal_kernel(*refs, packed=packed, first=first, groups=groups, scale=scale),
        out_shape=(
            jax.ShapeDtypeStruct(forcing.shape, F32),
            jax.ShapeDtypeStruct((rows, width), BF16),
            jax.ShapeDtypeStruct((2, rows, width), BF16),
            half,
            half,
        ),
        in_specs=specs,
        out_specs=(anywhere, vmem, vmem, vmem, vmem),
        scratch_shapes=[
            pltpu.VMEM((count, LANES), BF16),
            pltpu.VMEM((count, LANES), BF16),
            pltpu.VMEM((2, 4 * rows, count), BF16),
            pltpu.VMEM((rows, width), F32),
            pltpu.VMEM((3, rows, width), BF16),
            pltpu.VMEM((rows, width), F32),
            pltpu.VMEM((4 * rows, width), BF16),
            pltpu.SemaphoreType.DMA((4,)),
            pltpu.SemaphoreType.DMA,
        ],
        input_output_aliases=aliases,
        compiler_params=pltpu.CompilerParams(vmem_limit_bytes=VMEM_BYTES),
        cost_estimate=pl.CostEstimate(
            flops=2 * 2 * 2 * 4 * rows * count * width,
            bytes_accessed=2 * 2 * count * width + 2 * 4 * 4 * rows * width,
            transcendentals=0,
        ),
        name="zonal",
    )(*operands)
    return grid, near, far, stay, leave


def settle_kernel(place, g1, g2, g3, before, grid, wide, sem):
    mine, offset = place[1], pl.multiple_of(place[2], 8)
    rows = g1.shape[0]
    copies = []
    for n, ref in enumerate((g1, g2, g3)):
        wide[n] = ref[...].astype(F32)
        target = grid.at[mine ^ (n + 1), pl.ds(offset, rows), :]
        copies.append(pltpu.make_async_copy(wide.at[n], target, sem.at[n]))
        copies[-1].start()
    for copy in copies:
        copy.wait()


def settle(place, pieces, grid):
    vmem, anywhere = pl.BlockSpec(memory_space=pltpu.VMEM), pl.BlockSpec(memory_space=pl.ANY)
    return pl.pallas_call(
        settle_kernel,
        out_shape=jax.ShapeDtypeStruct(grid.shape, F32),
        in_specs=[pl.BlockSpec(memory_space=pltpu.SMEM), vmem, vmem, vmem, anywhere],
        out_specs=anywhere,
        scratch_shapes=[pltpu.VMEM((3,) + pieces[0].shape, F32), pltpu.SemaphoreType.DMA((3,))],
        input_output_aliases={4: 0},
        compiler_params=pltpu.CompilerParams(vmem_limit_bytes=VMEM_BYTES),
        name="settle",
    )(place, *pieces, grid)


def swap(value, axis, bit):
    pairs = [(n, n ^ bit) for n in range(lax.axis_size(axis))]
    return lax.ppermute(value, axis, pairs)


def add(*values):
    return sum(v.astype(F32) for v in values).astype(BF16)


def spread_lon(near, far):
    arrived = swap(far, "lon", 2)
    return swap(near, "lon", 1), arrived[0], swap(arrived[1], "lon", 1)


def pieces_of(arrays):
    kept, one, two, three = arrays
    return [kept[0], one[0], two[0], two[2], three[0], three[1], three[2], three[3]]


class Turns:
    def __init__(self):
        self.last = None

    def hold(self, values):
        return lax.optimization_barrier((values, self.last))[0]

    def run(self, step, *inputs):
        if self.last is not None:
            inputs, _ = lax.optimization_barrier((inputs, self.last))
        found = step(*inputs)
        self.last = jax.tree.leaves(found)[-1]
        return found


def exchange_lat(run, stay, leave, bits):
    one = swap(leave, "lat", bits[0])
    yield
    two = swap(run(lambda s, a: jnp.concatenate([s[2:], a[2:]]), stay, one), "lat", bits[1])
    yield
    leave = run(lambda s, a, b: jnp.stack([s[1], a[1], b[1], b[3]]), stay, one, two)
    three = swap(leave, "lat", bits[2])
    return stay, one, two, three


def fast_plan(spec, legendre, row_waves, forcing):
    groups, lon_size = lax.axis_size("lat"), lax.axis_size("lon")
    fields, _, slots, _ = spec.shape
    half_lats, band, width = legendre.shape[2], row_waves.shape[0], forcing.shape[2]
    per_pair, odd = divmod(2 * band, LANES)
    if (groups, lon_size, fields) != (8, 4, 4) or odd or per_pair != 5:
        return None
    if slots % STEP or half_lats != 4 * band or width % 256 or 2 * slots % STEP:
        return None
    pairs = range(half_lats // (2 * band))
    full = [
        [t for p in pairs for t in (per_pair * p + n, per_pair * (p + 1) - 1 - n)]
        for n in range(per_pair // 2)
    ]
    return [per_pair * p + per_pair // 2 for p in pairs], full


def body(spec, legendre, wave_pairs, row_waves, forcing, helm_coef):
    plan = fast_plan(spec, legendre, row_waves, forcing)
    if plan is None:
        return plain_body(spec, legendre, wave_pairs, row_waves, forcing, helm_coef)
    shared_tiles, full_tiles = plan
    groups = lax.axis_size("lat")
    lat_id, lon_id = lax.axis_index("lat"), lax.axis_index("lon")
    fields, _, slots, col_width = spec.shape
    band, seg_width = row_waves.shape[0], forcing.shape[2]
    length = seg_width * lax.axis_size("lon")
    top = groups // 2

    my_pairs = lax.dynamic_slice_in_dim(wave_pairs, lat_id * slots, slots)
    columns = lon_id * col_width + jnp.arange(col_width, dtype=jnp.int32)
    first_part, second_part, parity, degree = column_info(my_pairs, columns)
    factors = jnp.stack(
        [first_part, second_part, parity * first_part, parity * second_part], axis=1
    )
    near = jnp.stack([lax.dynamic_index_in_dim(spec, lon_id ^ d, 0, False) for d in range(4)])
    near = jnp.transpose(near.astype(BF16), (2, 0, 1, 3)).reshape(slots, 1, 2 * fields, col_width)
    mix = (factors[:, :, None].astype(BF16) * near).reshape(slots, 8 * fields, col_width)
    divisor = 1.0 + helm_coef[:, None, None] * (degree * (degree + 1.0))[None]
    inverse = (first_part + second_part)[None] / divisor

    grouped = wave_pairs.reshape(groups, slots)
    near_pairs = jnp.stack(
        [lax.dynamic_index_in_dim(grouped, lat_id ^ e, 0, False) for e in SOURCES]
    )
    waves = jnp.stack([near_pairs, M - 1 - near_pairs], axis=1).reshape(-1)
    quarter = waves[None] * (lon_id ^ jnp.arange(4, dtype=jnp.int32))[:, None] % 4
    cosine = jnp.where(quarter == 0, 1, jnp.where(quarter == 2, -1, 0))
    sine = jnp.where(quarter == 1, 1, jnp.where(quarter == 3, -1, 0))
    turns = jnp.stack([cosine, sine], axis=1).reshape(8, -1).astype(F32)

    south = lat_id >= top
    north = jnp.where(south, groups - 1 - lat_id, lat_id)
    row = jnp.arange(LANES, dtype=jnp.int32)
    place = jnp.stack([lat_id, lon_id])
    chunks = [(full_tiles[0], False, 0), (shared_tiles, True, 0), (full_tiles[1], False, 1)]
    setups, starts = [], []
    for tiles, packed, n in chunks:
        rows = HALF if packed else LANES
        start = band - rows if packed else n * LANES
        start = jnp.where(north % 2 == 0, start, band - rows - start)
        start = jnp.where(south, band - rows - start, start)
        mirrored = jnp.where(south, rows - 1 - row[:rows], row[:rows])
        if packed:
            target = HALF * jnp.arange(2)[:, None] + mirrored[None]
            flip = target[..., None] == row
            spread = jnp.concatenate([flip, flip], axis=1).astype(BF16)
        else:
            flip = mirrored[:, None] == row
            spread = jnp.zeros((8, LANES), BF16)
        kept = lax.dynamic_slice_in_dim(row_waves, start, rows)
        kept = jnp.sum(jnp.where(flip, kept[:, None], 0), axis=tuple(range(flip.ndim - 1)))
        starts.append(start)
        setups.append(((flip.astype(BF16), spread, kept[None].astype(jnp.int32))))

    def far_rows(forcing, start, rows):
        near, *far = [
            lax.dynamic_slice(forcing, (lon_id ^ d, start, 0), (1, rows, seg_width))[0].astype(BF16)
            for d in (1, 2, 3)
        ]
        return near, jnp.stack(far)

    split = [LANES, band - LANES]
    after_first = jnp.where(starts[0] == 0, LANES, 0)
    offsets = [jnp.zeros_like(starts[0])] + [s - after_first for s in starts[1:]]
    spots = [
        jnp.stack([lat_id, lon_id, s, o]).astype(jnp.int32) for s, o in zip(starts, offsets)
    ]
    turn = Turns()
    run = turn.run
    first_force = spread_lon(*run(lambda f: far_rows(f, starts[0], split[0]), forcing))
    state = {"grid": None, "total": None, "force": None, "table": None, "first": first_force}

    def chunk_steps(n):
        tiles, packed, _ = chunks[n]
        keep, send = run(
            lambda p, m, l: up_chunk(p, m, l, tiles, packed, groups, 0.5 / math.sqrt(M)), place, mix, legendre
        )
        yield
        other_far, other_own = swap(send[1], "lon", 1), swap(send[0], "lon", 1)
        if n == 2:
            keep, state["first"] = lax.optimization_barrier((keep, state["first"]))
        away = swap(run(lambda k, o: add(k[1], o), keep, other_far), "lon", 2)
        yield
        half = groups // 2
        stay, leave = run(
            lambda k, o, a: (add(k[0, :half], o[:half], a[:half]), add(k[0, half:], o[half:], a[half:])),
            keep, other_own, away,
        )
        arrays = yield from exchange_lat(run, stay, leave, (4, 2, 1))
        yield
        force = state["force"] if n else state["first"]
        grid, near, far, stay, leave = run(
            lambda *a: zonal_chunk(
                spots[n], a[:4], a[4], setups[n], waves[:, None], turns, forcing, a[5:], state["grid"], packed, 1.0 / length
            ),
            *arrays, state["table"], *force,
        )
        state["grid"] = grid
        settled.append((spots[n], (near, far) if n == 2 else spread_lon(near, far)))
        arrays = yield from exchange_lat(run, stay, leave, (1, 2, 4))
        yield
        own = run(lambda *a: jnp.stack(pieces_of(a)), *arrays)
        across = swap(own, "lon", 2)
        fans = own, swap(own, "lon", 1), across, swap(across, "lon", 1)
        yield
        state["total"] = run(
            lambda *a: down_chunk(
                place, a, legendre, factors, state["total"], spec if n == 2 else None,
                inverse if n == 2 else None, tiles, packed, groups,
            ),
            *fans,
        )
        yield

    settled = []
    walks = [chunk_steps(n) for n in range(3)]
    for step in STEPS:
        if step is None:
            state["table"] = run(lambda w: make_table(w, 0, seg_width, length, groups), waves)
        elif step == "force":
            state["force"] = spread_lon(*run(lambda f: far_rows(f, after_first, split[1]), forcing))
        elif step == "grid":
            settled[2] = settled[2][0], spread_lon(*turn.hold(settled[2][1]))
        elif step < 3:
            next(walks[step])
        else:
            spot, parts = settled[step - 3]
            state["grid"] = run(lambda *a: settle(spot, a, state["grid"]), *parts)
    return state["grid"], state["total"]


def solution(mesh):
    return jax.shard_map(
        body,
        mesh=mesh,
        in_specs=(
            P(None, None, "lat", "lon"),
            P("lat", "lon", None),
            P(),
            P("lat"),
            P(None, "lat", "lon"),
            P(),
        ),
        out_specs=(P(None, "lat", "lon"), P(None, None, "lat", "lon")),
        check_vma=False,
    )
```
